32 devices in a mesh: dp: 8 (over y, x, core), tensor: 4 (over z).
Axes of the slice: x: 2, y: 2, z: 4, core: 2. Of those that a mesh axis runs over, the one named last changes fastest.
Arguments:
- block_input: bfloat16 [8, 1024, 768], P('dp', 'tensor'), may hold values from -6 to 6
- w_q: bfloat16 [768, 768], P('dp', 'tensor'), may hold values from -0.21875 to 0.21875
- w_k: bfloat16 [768, 768], P('dp', 'tensor'), may hold values from -0.21875 to 0.21875
- w_v: bfloat16 [768, 768], P('dp', 'tensor'), may hold values from -0.21875 to 0.21875
- w_o: bfloat16 [768, 768], P('tensor', 'dp'), may hold values from -1.75 to 1.75
- b_q: float32 [768], P('tensor'), may hold values from -3 to 3
- b_v: float32 [768], P('tensor'), may hold values from -3 to 3
- b_o: float32 [768], replicated, may hold values from -2 to 2
- w_1: bfloat16 [768, 3072], P('dp', 'tensor'), may hold values from -0.21875 to 0.21875
- b_1: float32 [3072], P('tensor'), may hold values from -3 to 3
- w_2: bfloat16 [3072, 768], P('tensor', 'dp'), may hold values from -0.109375 to 0.109375
- b_2: float32 [768], replicated, may hold values from -2 to 2
- gain_1: float32 [768], replicated, may hold values from 0.25 to 1.75
- shift_1: float32 [768], replicated, may hold values from -2 to 2
- gain_2: float32 [768], replicated, may hold values from 0.25 to 1.75
- shift_2: float32 [768], replicated, may hold values from -2 to 2
- cotangent: bfloat16 [8, 1024, 768], P('dp', 'tensor'), may hold values from -6 to 6
Outputs:
- block_output: bfloat16 [8, 1024, 768], P('dp', 'tensor')
- grad_x: bfloat16 [8, 1024, 768], P('dp', 'tensor')
- grad_w_q: float32 [768, 768], P('dp', 'tensor')
- grad_w_k: float32 [768, 768], P('dp', 'tensor')
- grad_w_v: float32 [768, 768], P('dp', 'tensor')
- grad_w_o: float32 [768, 768], P('tensor', 'dp')
- grad_b_q: float32 [768], replicated
- grad_b_v: float32 [768], replicated
- grad_b_o: float32 [768], replicated
- grad_w_1: float32 [768, 3072], P('dp', 'tensor')
- grad_b_1: float32 [3072], replicated
- grad_w_2: float32 [3072, 768], P('tensor', 'dp')
- grad_b_2: float32 [768], replicated
- grad_gain_1: float32 [768], replicated
- grad_shift_1: float32 [768], replicated
- grad_gain_2: float32 [768], replicated
- grad_shift_2: float32 [768], replicated
The draws below stay inside these ranges and needn't reach their ends.
All inputs are finite; a program needn't handle non-finite values.
Results may differ from the reference program's by a relative error of at most 0.019.
Values may be sent and summed in bfloat16 or wider, within the bound.
A program may use at most 128 MiB of HBM per device.

```python
import jax
import jax.numpy as jnp
from jax import lax

D = 768
HEAD = 64
FF = 3072
SEQ = 1024
QBLK = 512
CLIPS = 8


def strengthened(values, key, source, target, parts, factor):
    def block_of(dim):
        return (jnp.arange(values.shape[dim]) // (values.shape[dim] // parts)).reshape((-1,) + (1,) * (values.ndim - 1 - dim))

    near = jax.random.permutation(key, parts)[block_of(target)]
    far = (block_of(target) + parts // 2) % parts
    return jnp.where((block_of(source) == near) | (block_of(source) == far), factor * values, values)


def level_of(stream_key, extent, cuts, least, largest):
    def one(dim, shards_of):
        steps = jax.random.uniform(jax.random.fold_in(jax.random.fold_in(stream_key, 6), dim), (shards_of,), jnp.float32, least / len(cuts), largest / len(cuts))
        return jnp.repeat(jnp.exp(steps), extent[dim] // shards_of).reshape((-1,) + (1,) * (len(extent) - dim - 1))

    loudness = one(*cuts[0])
    for cut in cuts[1:]:
        loudness = loudness * one(*cut)
    return loudness


def scatter_about(rng, shape, deviation, bound, split=(), held_as=jnp.bfloat16):
    level = level_of(rng, shape, split, -0.22, 0.18) if split else 1.0
    values = jax.random.normal(rng, shape, jnp.float32) * deviation * level
    return jnp.minimum(jnp.maximum(values, -bound), bound).astype(held_as)


def heavy_noise(key, extent, scale, most, pieces, heavy, held_as=jnp.bfloat16):
    values = scale * jax.random.normal(key, extent, jnp.float32)
    if pieces:
        values = values * level_of(key, extent, pieces, -0.22, 0.18)
    return jnp.clip(strengthened(values, jax.random.fold_in(key, 3), *heavy), -most, most).astype(held_as)


def setup_inputs(seed: int = 0) -> dict:
    key_of = jax.random.split(jax.random.key(seed), 18)
    return {
        "block_input": scatter_about(key_of[0], (CLIPS, SEQ, D), 1.0, 6.0, ((0, 8), (1, 4))),
        "w_q": scatter_about(key_of[1], (D, D), D ** -0.5, 0.21875, ((0, 8), (1, 4))),
        "w_k": scatter_about(key_of[2], (D, D), D ** -0.5, 0.21875, ((0, 8), (1, 4))),
        "w_v": scatter_about(key_of[3], (D, D), D ** -0.5, 0.21875, ((0, 8), (1, 4))),
        "w_o": scatter_about(key_of[4], (D, D), (max(1, D * 16 // SEQ)) ** -0.5, 1.75, ((0, 4), (1, 8))),
        "b_q": scatter_about(key_of[5], (D,), 0.5, 3.0, ((0, 4),), jnp.float32),
        "b_v": scatter_about(key_of[6], (D,), 0.5, 3.0, ((0, 4),), jnp.float32),
        "b_o": scatter_about(key_of[7], (D,), 0.3, 2.0, (), jnp.float32),
        "w_1": scatter_about(key_of[8], (D, FF), D ** -0.5, 0.21875, ((0, 8), (1, 4))),
        "b_1": scatter_about(key_of[9], (FF,), 0.5, 3.0, ((0, 4),), jnp.float32),
        "w_2": scatter_about(key_of[10], (FF, D), FF ** -0.5, 0.109375, ((0, 4), (1, 8))),
        "b_2": scatter_about(key_of[11], (D,), 0.3, 2.0, (), jnp.float32),
        "gain_1": jnp.clip(1.0 + 0.15 * jax.random.normal(key_of[12], (D,), jnp.float32), 0.25, 1.75),
        "shift_1": scatter_about(key_of[13], (D,), 0.3, 2.0, (), jnp.float32),
        "gain_2": jnp.clip(1.0 + 0.15 * jax.random.normal(key_of[14], (D,), jnp.float32), 0.25, 1.75),
        "shift_2": scatter_about(key_of[15], (D,), 0.3, 2.0, (), jnp.float32),
        "cotangent": heavy_noise(key_of[16], (CLIPS, SEQ, D), 1.0, 6.0, ((0, 8), (1, 4)), (0, 2, 8, 2.0)),
    }


EPS = 1e-05
precise_mode = lax.Precision.HIGHEST

@jax.custom_vjp
def low(v):
    return lax.optimization_barrier(v.astype(jnp.bfloat16)).astype(jnp.float32)

@jax.custom_vjp
def low_back(v):
    return v

def low_keep(v):
    return (low(v), None)

def low_pass(kept, grad):
    return (grad,)

def back_keep(v):
    return (v, None)

def back_low(kept, grad):
    return (low(grad),)
low.defvjp(low_keep, low_pass)
low_back.defvjp(back_keep, back_low)

def product(left_side, right_side):
    return jnp.dot(left_side, right_side, precision=precise_mode, preferred_element_type=jnp.float32)

def layer_norm(activity, gain_vec, shift_vec):
    average = lax.optimization_barrier(jnp.mean(activity, axis=-1, keepdims=True))
    centred = activity - average
    spread = lax.optimization_barrier(jnp.mean(centred * centred, axis=-1, keepdims=True))
    return centred * lax.rsqrt(spread + EPS) * gain_vec + shift_vec

def attention(query_rows, key_rows, value_rows):
    length = query_rows.shape[0]
    head_count = query_rows.shape[1] // HEAD
    query_blocks = query_rows.reshape(length // QBLK, QBLK, head_count, HEAD)
    key_heads = key_rows.reshape(length, head_count, HEAD)
    value_heads = value_rows.reshape(length, head_count, HEAD)

    def one_block(query_block):
        scores = jnp.einsum('qhd,khd->hqk', query_block, key_heads, precision=precise_mode) * HEAD ** (-0.5)
        scores = low_back(scores)
        weights = low(jax.nn.softmax(scores, axis=-1))
        return jnp.einsum('hqk,khd->qhd', weights, value_heads, precision=precise_mode)
    mixed = lax.map(jax.checkpoint(one_block), query_blocks)
    return mixed.reshape(length, head_count * HEAD)

def forward(layer_in, w_q, w_k, w_v, w_o, b_q, b_v, b_o, w_1, b_1, w_2, b_2, gain_1, shift_1, gain_2, shift_2):
    normed = low(layer_norm(layer_in, gain_1, shift_1))
    query_rows = low(low_back(product(normed, w_q) + b_q))
    key_rows = low(low_back(product(normed, w_k)))
    value_rows = low(low_back(product(normed, w_v) + b_v))
    mixed = low(low_back(attention(query_rows, key_rows, value_rows)))
    middle = layer_in + low_back(product(mixed, w_o)) + b_o
    normed_two = low(layer_norm(middle, gain_2, shift_2))
    hidden = low_back(product(normed_two, w_1) + b_1)
    active = low(jax.nn.gelu(hidden, approximate=False))
    return middle + low_back(product(active, w_2)) + b_2

def reference(block_input, w_q, w_k, w_v, w_o, b_q, b_v, b_o, w_1, b_1, w_2, b_2, gain_1, shift_1, gain_2, shift_2, cotangent):
    params = tuple((item.astype(jnp.float32) for item in (w_q, w_k, w_v, w_o, b_q, b_v, b_o, w_1, b_1, w_2, b_2, gain_1, shift_1, gain_2, shift_2)))

    def clip_step(running, clip_pair):
        clip_in, clip_cot = clip_pair
        result, pullback = jax.vjp(forward, clip_in.astype(jnp.float32), *params)
        gradients = pullback(clip_cot.astype(jnp.float32))
        running = tuple((total + piece for total, piece in zip(running, gradients[1:])))
        return (running, (result.astype(jnp.bfloat16), gradients[0].astype(jnp.bfloat16)))
    zero_start = tuple((jnp.zeros_like(item) for item in params))
    running, (outputs, input_grads) = lax.scan(clip_step, zero_start, (block_input, cotangent))
    g_wq, g_wk, g_wv, g_wo, g_bq, g_bv, g_bo, g_w1, g_b1, g_w2, g_b2, g_g1, g_s1, g_g2, g_s2 = running
    return (outputs, input_grads, g_wq, g_wk, g_wv, g_wo, g_bq, g_bv, g_bo, g_w1, g_b1, g_w2, g_b2, g_g1, g_s1, g_g2, g_s2)
```

```python
import jax
import jax.numpy as jnp
from jax import lax
from jax.sharding import PartitionSpec as P

HEAD = 64
EPS = 1e-05
BF = jnp.bfloat16
F32 = jnp.float32


def normalize(activity, gain_vec, shift_vec):
    average = jnp.mean(activity, axis=-1, keepdims=True)
    centred = activity - average
    inverse = lax.rsqrt(jnp.mean(centred * centred, axis=-1, keepdims=True) + EPS)
    normed = centred * inverse
    return (normed * gain_vec + shift_vec, normed, inverse)


def normalize_back(upstream, normed, inverse, gain_vec):
    scaled = upstream * gain_vec
    first = jnp.mean(scaled, axis=-1, keepdims=True)
    second = jnp.mean(scaled * normed, axis=-1, keepdims=True)
    grad_in = inverse * (scaled - first - normed * second)
    return (grad_in, jnp.sum(upstream * normed, axis=0), jnp.sum(upstream, axis=0))


def einsum(spec, left_side, right_side):
    return jnp.einsum(spec, left_side, right_side, preferred_element_type=F32)


def split_heads(activity):
    return activity.reshape(activity.shape[0], -1, HEAD)


def attend_forward(query, key, value):
    scale = HEAD ** (-0.5)
    scores = einsum("qhd,khd->hqk", split_heads(query), split_heads(key)) * scale
    peak = jnp.max(scores, axis=-1, keepdims=True)
    exp_scores = jnp.exp(scores - peak)
    total = jnp.sum(exp_scores, axis=-1, keepdims=True)
    weights = (exp_scores / total).astype(BF)
    mixed = einsum("hqk,khd->qhd", weights, split_heads(value))
    return mixed.reshape(query.shape).astype(BF), peak + jnp.log(total)


def attend_backward(query, key, value, grad_mixed, totals):
    scale = HEAD ** (-0.5)
    query_h, key_h, value_h, grad_h = map(split_heads, (query, key, value, grad_mixed))
    probs = jnp.exp(einsum("qhd,khd->hqk", query_h, key_h) * scale - totals)
    grad_value = einsum("hqk,qhd->khd", probs.astype(BF), grad_h)
    grad_probs = einsum("qhd,khd->hqk", grad_h, value_h)
    inner = jnp.sum(probs * grad_probs, axis=-1, keepdims=True)
    grad_scores = (probs * (grad_probs - inner)).astype(BF)
    grad_query = einsum("hqk,khd->qhd", grad_scores, key_h) * scale
    grad_key = einsum("hqk,qhd->khd", grad_scores, query_h) * scale
    return (
        grad_query.reshape(query.shape).astype(BF),
        grad_key.reshape(key.shape).astype(BF),
        grad_value.reshape(key.shape).astype(BF),
    )


ALL = ("tensor", "dp")


def gather_weights(shard, tensor_count):
    full = lax.all_gather(shard, ALL, axis=0, tiled=True)
    return full.reshape(tensor_count, -1, shard.shape[1])


def scatter_weights(full):
    return lax.psum_scatter(
        full.reshape(-1, full.shape[-1]), ALL, scatter_dimension=0, tiled=True
    ).astype(F32)


def local(
    block_input,
    w_q,
    w_k,
    w_v,
    w_o,
    b_q,
    b_v,
    b_o,
    w_1,
    b_1,
    w_2,
    b_2,
    gain_1,
    shift_1,
    gain_2,
    shift_2,
    cotangent,
):
    tensor_count = lax.axis_size("tensor")
    inputs = block_input[0].astype(F32)
    width = inputs.shape[1]
    head_cols = w_q.shape[1]
    normed_1, plain_1, inverse_1 = normalize(inputs, gain_1, shift_1)
    own_1 = normed_1.astype(BF)
    full_1 = lax.all_gather(own_1, "tensor", axis=0, tiled=True)
    packed = gather_weights(jnp.concatenate([w_q, w_k, w_v, w_o.T], axis=1), tensor_count)
    biases = lax.all_gather(jnp.concatenate([b_q, b_v, b_1]), "tensor", axis=0)
    up_w = gather_weights(w_1, tensor_count)
    down_wt = gather_weights(w_2.T, tensor_count)
    packed = packed.reshape(tensor_count, width, 4, head_cols)
    query_w, key_w, value_w, out_wt = packed.transpose(2, 1, 0, 3).reshape(4, width, -1)
    bias_q = biases[:, :head_cols].reshape(-1)
    bias_v = biases[:, head_cols : 2 * head_cols].reshape(-1)
    bias_1 = biases[:, 2 * head_cols :]

    query = (einsum("fd,dc->fc", own_1, query_w) + bias_q).astype(BF)
    key = einsum("fd,dc->fc", full_1, key_w).astype(BF)
    value = (einsum("fd,dc->fc", full_1, value_w) + bias_v).astype(BF)
    mixed, totals = attend_forward(query, key, value)
    middle = inputs + einsum("fc,dc->fd", mixed, out_wt) + b_o
    normed_2, plain_2, inverse_2 = normalize(middle, gain_2, shift_2)
    own_2 = normed_2.astype(BF)
    hidden = einsum("fd,tdc->tfc", own_2, up_w) + bias_1[:, None, :]
    cdf = 0.5 * (1.0 + lax.erf(hidden * 0.7071067811865476))
    active = (hidden * cdf).astype(BF)
    result = middle + einsum("tfc,tdc->fd", active, down_wt) + b_2
    upstream = cotangent[0]
    grad_active = einsum("fd,tdc->tfc", upstream, down_wt)
    pdf = jnp.exp(-0.5 * hidden * hidden) * 0.3989422804014327
    grad_hidden = (grad_active * (cdf + hidden * pdf)).astype(BF)
    grad_up = einsum("fd,tfc->tdc", own_2, grad_hidden).astype(BF)
    grad_down = einsum("fd,tfc->tdc", upstream, active).astype(BF)
    sum_1 = jnp.sum(grad_hidden.astype(F32), axis=1).reshape(-1)
    shard_up = scatter_weights(grad_up)
    shard_down = scatter_weights(grad_down).T
    grad_norm_2 = einsum("tfc,tdc->fd", grad_hidden, up_w)
    down_in = upstream.astype(F32)
    grad_mid_norm, gain2_grad, shift2_grad = normalize_back(grad_norm_2, plain_2, inverse_2, gain_2)
    grad_middle = down_in + grad_mid_norm
    grad_mid = grad_middle.astype(BF)
    grad_mixed = einsum("fd,dc->fc", grad_mid, out_wt).astype(BF)
    grad_query, grad_key, grad_value = attend_backward(query, key, value, grad_mixed, totals)
    part = einsum("fc,dc->fd", grad_key, key_w) + einsum("fc,dc->fd", grad_value, value_w)
    scattered = lax.psum_scatter(part.astype(BF), "tensor", scatter_dimension=0, tiled=True)
    grad_out = einsum("fd,fc->dc", grad_mid, mixed)
    grad_qw = einsum("fd,fc->dc", own_1, grad_query)
    grad_kw = einsum("fd,fc->dc", full_1, grad_key)
    grad_vw = einsum("fd,fc->dc", full_1, grad_value)
    grads = jnp.stack([grad_qw, grad_kw, grad_vw, grad_out]).astype(BF)
    grads = grads.reshape(4, width, tensor_count, head_cols).transpose(2, 1, 0, 3)
    shard = scatter_weights(grads.reshape(tensor_count, width, -1))
    shard_qw, shard_kw, shard_vw, shard_ow = jnp.split(shard, 4, axis=1)
    grad_norm_1 = scattered.astype(F32) + einsum("fc,dc->fd", grad_query, query_w)
    grad_in_norm, gain1_grad, shift1_grad = normalize_back(grad_norm_1, plain_1, inverse_1, gain_1)
    grad_input = grad_middle + grad_in_norm
    pieces = [
        jnp.sum(grad_query.astype(F32), axis=0),
        jnp.sum(grad_value.astype(F32), axis=0),
        jnp.sum(grad_middle, axis=0),
        sum_1,
        jnp.sum(down_in, axis=0),
        gain1_grad,
        shift1_grad,
        gain2_grad,
        shift2_grad,
    ]
    sums = lax.psum(jnp.concatenate(pieces), ALL)
    ends = []
    for piece in pieces:
        ends.append((ends[-1] if ends else 0) + piece.shape[0])
    sum_bq, sum_bv, sum_bo, sum_b1, sum_b2, sum_g1, sum_s1, sum_g2, sum_s2 = jnp.split(
        sums, ends[:-1]
    )
    return (
        result.astype(BF)[None],
        grad_input.astype(BF)[None],
        shard_qw,
        shard_kw,
        shard_vw,
        shard_ow.T,
        sum_bq,
        sum_bv,
        sum_bo,
        shard_up,
        sum_b1,
        shard_down,
        sum_b2,
        sum_g1,
        sum_s1,
        sum_g2,
        sum_s2,
    )


def solution(mesh):
    in_specs = (
        P("dp", "tensor", None),
        P("dp", "tensor"),
        P("dp", "tensor"),
        P("dp", "tensor"),
        P("tensor", "dp"),
        P("tensor"),
        P("tensor"),
        P(),
        P("dp", "tensor"),
        P("tensor"),
        P("tensor", "dp"),
        P(),
        P(),
        P(),
        P(),
        P(),
        P("dp", "tensor", None),
    )
    out_specs = (
        P("dp", "tensor", None),
        P("dp", "tensor", None),
        P("dp", "tensor"),
        P("dp", "tensor"),
        P("dp", "tensor"),
        P("tensor", "dp"),
        P(),
        P(),
        P(),
        P("dp", "tensor"),
        P(),
        P("tensor", "dp"),
        P(),
        P(),
        P(),
        P(),
        P(),
    )
    return jax.shard_map(local, mesh=mesh, in_specs=in_specs, out_specs=out_specs, check_vma=False)
```

```python
import jax
import jax.numpy as jnp
from jax import lax
from jax.experimental import pallas as pl
from jax.experimental.pallas import tpu as pltpu
from jax.sharding import PartitionSpec as P

HEAD = 64
EPS = 1e-05
BF = jnp.bfloat16
F32 = jnp.float32


def normalize(activity, gain_vec, shift_vec):
    average = jnp.mean(activity, axis=-1, keepdims=True)
    centred = activity - average
    inverse = lax.rsqrt(jnp.mean(centred * centred, axis=-1, keepdims=True) + EPS)
    normed = centred * inverse
    return (normed * gain_vec + shift_vec, normed, inverse)


def normalize_back(upstream, normed, inverse, gain_vec):
    scaled = upstream * gain_vec
    first = jnp.mean(scaled, axis=-1, keepdims=True)
    second = jnp.mean(scaled * normed, axis=-1, keepdims=True)
    grad_in = inverse * (scaled - first - normed * second)
    return (grad_in, jnp.sum(upstream * normed, axis=0), jnp.sum(upstream, axis=0))


def einsum(spec, left_side, right_side):
    return jnp.einsum(spec, left_side, right_side, preferred_element_type=F32)


def heads(activity):
    return activity.reshape(activity.shape[:2] + (-1, HEAD))


def attend_forward(query, key, value):
    scale = HEAD ** (-0.5)
    scores = einsum("tqhd,tkhd->thqk", heads(query), heads(key)) * scale
    peak = jnp.max(scores, axis=-1, keepdims=True)
    exp_scores = jnp.exp(scores - peak)
    total = jnp.sum(exp_scores, axis=-1, keepdims=True)
    weights = (exp_scores / total).astype(BF)
    mixed = einsum("thqk,tkhd->tqhd", weights, heads(value))
    return mixed.reshape(query.shape).astype(BF), peak + jnp.log(total)


def attend_backward(query, key, value, grad_mixed, totals):
    scale = HEAD ** (-0.5)
    query_h, key_h, value_h, grad_h = map(heads, (query, key, value, grad_mixed))
    probs = jnp.exp(einsum("tqhd,tkhd->thqk", query_h, key_h) * scale - totals)
    grad_value = einsum("thqk,tqhd->tkhd", probs.astype(BF), grad_h)
    grad_probs = einsum("tqhd,tkhd->thqk", grad_h, value_h)
    inner = jnp.sum(probs * grad_probs, axis=-1, keepdims=True)
    grad_scores = (probs * (grad_probs - inner)).astype(BF)
    grad_query = einsum("thqk,tkhd->tqhd", grad_scores, key_h) * scale
    grad_key = einsum("thqk,tqhd->tkhd", grad_scores, query_h) * scale
    return (
        grad_query.reshape(query.shape).astype(BF),
        grad_key.reshape(key.shape).astype(BF),
        grad_value.reshape(key.shape).astype(BF),
    )


ALL = ("tensor", "dp")
MESH = pl.DeviceIdType.MESH


def place():
    d, t = lax.axis_index("dp"), lax.axis_index("tensor")
    return d, t, d // 4, (d // 2) % 2, d % 2


def slot_order(t):
    far = jnp.where(t < 2, 3, 0)
    second = jnp.where(t == 0, 1, jnp.where(t == 3, 2, t - 1))
    third = jnp.where(t == 0, 2, jnp.where(t == 3, 1, t + 1))
    return [t, second, third, far]


def greet(peers, t, extra):
    barrier = pltpu.get_barrier_semaphore()
    for peer in peers:
        pl.semaphore_signal(barrier, inc=1, device_id=peer, device_id_type=MESH)
    d = lax.axis_index("dp")

    @pl.when(t > 0)
    def _():
        pl.semaphore_signal(barrier, inc=1, device_id=(d, t - 1), device_id_type=MESH)

    @pl.when(t < 3)
    def _():
        pl.semaphore_signal(barrier, inc=1, device_id=(d, t + 1), device_id_type=MESH)

    pl.semaphore_wait(
        barrier, len(peers) + jnp.where(t > 0, 1, 0) + jnp.where(t < 3, 1, 0)
    )


def remote(src, dst, send, recv, peer):
    return pltpu.make_async_remote_copy(
        src_ref=src, dst_ref=dst, send_sem=send, recv_sem=recv, device_id=peer, device_id_type=MESH
    )


def gather_kernel(*refs):
    ins, outs = refs[:5], refs[5:10]
    local_sem, line_send, line_recv, send, recv = refs[10:]
    d, t, y, x, c = place()
    weights = outs[:3]
    half = ins[0].shape[0] // 2
    first, last = pl.ds(0, half), pl.ds(half, half)
    x_peer = (d + 2 - 4 * x, t)
    y_peer = (d + 4 - 8 * y, t)
    core_peer = (d + 1 - 2 * c, t)

    own = [out.at[t, y, x, c] for out in weights] + [out.at[t] for out in outs[3:]]
    copies = [pltpu.make_async_copy(a, b, local_sem.at[i]) for i, (a, b) in enumerate(zip(ins, own))]
    for copy in copies:
        copy.start()
    greet([x_peer, y_peer, core_peer], t, 0)
    for copy in copies:
        copy.wait()
    order = slot_order(t)

    def line(slot, way):
        peer = (d, jnp.minimum(t + 1, 3)) if way == 0 else (d, jnp.maximum(t - 1, 0))
        spots = [outs[3].at[slot], outs[4].at[slot]] + [out.at[slot, y, x, c] for out in weights]
        return [
            remote(spot, spot, line_send.at[way, slot, i], line_recv.at[slot, i], peer)
            for i, spot in enumerate(spots)
        ]

    def plane(slot, stage):
        made = []
        for g, out in enumerate(weights):
            if stage == 0:
                spots = [(0, out.at[slot, y, x, c, first], x_peer), (1, out.at[slot, y, x, c, last], y_peer)]
            elif stage == 1:
                spots = [(2, out.at[slot, y, :, c, first], y_peer), (3, out.at[slot, :, x, c, last], x_peer)]
            else:
                spots = [(4, out.at[slot, :, :, c], core_peer)]
            for k, spot, peer in spots:
                made.append(remote(spot, spot, send.at[slot, g, k], recv.at[slot, g, k], peer))
        return made

    def landed(slot, stage):
        for g, out in enumerate(weights):
            if stage == 0:
                spots = [(0, out.at[slot, y, 1 - x, c, first], x_peer), (1, out.at[slot, 1 - y, x, c, last], y_peer)]
            elif stage == 1:
                spots = [(2, out.at[slot, 1 - y, :, c, first], y_peer), (3, out.at[slot, :, 1 - x, c, last], x_peer)]
            else:
                spots = [(4, out.at[slot, :, :, 1 - c], core_peer)]
            for k, spot, peer in spots:
                remote(spot, spot, send.at[slot, g, k], recv.at[slot, g, k], peer).wait_recv()

    def both_ways(slot, act):
        @pl.when((slot <= t) & (t < 3))
        def _():
            for copy in line(slot, 0):
                act(copy)

        @pl.when((slot >= t) & (t > 0))
        def _():
            for copy in line(slot, 1):
                act(copy)

    for step in range(7):
        if step < 4:
            slot = order[step]
            if step:
                for copy in line(slot, 0):
                    copy.wait_recv()
            both_ways(slot, lambda copy: copy.start())
            for copy in plane(slot, 0):
                copy.start()
        for stage in (0, 1):
            if 0 <= step - 1 - stage < 4:
                slot = order[step - 1 - stage]
                landed(slot, stage)
                for copy in plane(slot, stage + 1):
                    copy.start()
        if 0 <= step - 3:
            landed(order[step - 3], 2)
    for slot in order:
        both_ways(slot, lambda copy: copy.wait_send())
        for stage in range(3):
            for copy in plane(slot, stage):
                copy.wait_send()


def gather_all(shards, own_1, bias):
    rows, width = shards[0].shape
    if (lax.axis_size("dp"), lax.axis_size("tensor")) != (8, 4):
        count = lax.axis_size("tensor")
        full = [lax.all_gather(w, ALL, axis=0, tiled=True).reshape(count, -1, width) for w in shards]
        return full, lax.all_gather(own_1, "tensor", axis=0, tiled=True), lax.all_gather(
            bias, "tensor", axis=0
        )
    any_spec = pl.BlockSpec(memory_space=pl.ANY)
    bias = jnp.pad(bias, (0, -bias.shape[0] % 1024)).reshape(-1, 128)
    dma = pltpu.SemaphoreType.DMA
    outs = pl.pallas_call(
        gather_kernel,
        out_shape=[jax.ShapeDtypeStruct((4, 2, 2, 2, rows, width), BF)] * 3
        + [
            jax.ShapeDtypeStruct((4,) + own_1.shape, BF),
            jax.ShapeDtypeStruct((4,) + bias.shape, F32),
        ],
        in_specs=[any_spec] * 5,
        out_specs=[any_spec] * 5,
        scratch_shapes=[dma((5,)), dma((2, 4, 5)), dma((4, 5)), dma((4, 3, 5)), dma((4, 3, 5))],
        compiler_params=pltpu.CompilerParams(collective_id=0, has_side_effects=True),
    )(*shards, own_1, bias)
    full = [w.reshape(4, 8 * rows, width) for w in outs[:3]]
    return full, outs[3].reshape(-1, width), outs[4].reshape(4, -1)


def scatter_kernel(*refs):
    grads, (part, own_part, plain, small) = refs[:3], refs[3:7]
    sums, total_1, total_s = refs[7:10]
    r1, ra0, ra1, rb, z_in, z_out, n_in, n_out, s_buf = refs[10:19]
    send, recv, z_send, z_recv, n_send, n_recv, s_send, s_recv = refs[19:]
    d, t, y, x, c = place()
    rows = sums.shape[1]
    half = rows // 2
    first, last = pl.ds(0, half), pl.ds(half, half)
    x_peer = (d + 2 - 4 * x, t)
    y_peer = (d + 4 - 8 * y, t)
    core_peer = (d + 1 - 2 * c, t)
    near_peer = (d, t + 1 - 2 * (t % 2))
    far_peer = (d, t + 2 - 4 * (t // 2))
    greet([x_peer, y_peer, core_peer, far_peer], t, 0)
    order = slot_order(t)[::-1]

    def core_copies(j):
        slot = order[j]
        return [
            remote(grads[g].at[slot, :, :, 1 - c], r1.at[j, g], send.at[j, g], recv.at[j, g], core_peer)
            for g in range(3)
        ]

    def a_copies(j):
        return [
            remote(r1.at[j, :, 1 - y, :, first], ra0.at[j], send.at[j, 3], recv.at[j, 3], y_peer),
            remote(r1.at[j, :, :, 1 - x, last], ra1.at[j], send.at[j, 4], recv.at[j, 4], x_peer),
        ]

    def b_copies(j):
        return [
            remote(ra0.at[j, :, 1 - x], rb.at[j, :, first], send.at[j, 5], recv.at[j, 5], x_peer),
            remote(ra1.at[j, :, 1 - y], rb.at[j, :, last], send.at[j, 6], recv.at[j, 6], y_peer),
        ]

    def ahead(slot):
        return jnp.where(slot > t, t + 1, t - 1), jnp.where(slot > t, 0, 1)

    def z_copy(j):
        slot = order[j]
        peer, way = ahead(slot)
        return remote(z_out.at[j], z_in.at[way, slot], z_send.at[j], z_recv.at[way, slot], (d, peer))

    def n_copy(j):
        slot = order[j]
        peer, way = ahead(slot)
        return remote(n_out.at[j], n_in.at[way, slot], n_send.at[j], n_recv.at[way, slot], (d, peer))

    def line_landed(buf, out, sem, peer_sem, slot, way):
        remote(out.at[0], buf.at[way, slot], peer_sem.at[0], sem.at[way, slot], near_peer).wait_recv()

    def add(a, b):
        return a.astype(F32) + b.astype(F32)

    for j in range(4):
        for copy in core_copies(j):
            copy.start()
    for step in range(6):
        if step < 3:
            slot = order[step]
            way = jnp.where(slot > t, 0, 1)
            fed = ((slot > t) & (t > 0)) | ((slot < t) & (t < 3))

            @pl.when(fed)
            def _():
                line_landed(n_in, n_out, n_recv, n_send, slot, way)
                n_out[step] = add(part[slot], n_in[way, slot]).astype(BF)

            @pl.when(jnp.logical_not(fed))
            def _():
                n_out[step] = part[slot]

            n_copy(step).start()
        if step < 4:
            j = step
            slot = order[j]
            for copy in core_copies(j):
                copy.wait_recv()

            @pl.loop(0, 4)
            def _(m):
                for g in range(3):
                    r1[j, g, m // 2, m % 2] = add(
                        r1[j, g, m // 2, m % 2], grads[g][slot, m // 2, m % 2, c]
                    ).astype(BF)

            for copy in a_copies(j):
                copy.start()
        if 0 <= step - 1 < 4:
            j = step - 1
            for copy in a_copies(j):
                copy.wait_recv()

            @pl.loop(0, 2)
            def _(m):
                for g in range(3):
                    ra0[j, g, m] = add(ra0[j, g, m], r1[j, g, y, m, first]).astype(BF)
                    ra1[j, g, m] = add(ra1[j, g, m], r1[j, g, m, x, last]).astype(BF)

            for copy in b_copies(j):
                copy.start()
        if 0 <= step - 2 < 4:
            j = step - 2
            slot = order[j]
            for copy in b_copies(j):
                copy.wait_recv()

            @pl.loop(0, 3)
            def _(g):
                z_out[j, g, first] = add(rb[j, g, first], ra0[j, g, x]).astype(BF)
                z_out[j, g, last] = add(rb[j, g, last], ra1[j, g, y]).astype(BF)

            if j < 3:
                way = jnp.where(slot > t, 0, 1)
                fed = ((slot > t) & (t > 0)) | ((slot < t) & (t < 3))

                @pl.when(fed)
                def _():
                    line_landed(z_in, z_out, z_recv, z_send, slot, way)

                    @pl.loop(0, 3)
                    def _(g):
                        z_out[j, g] = add(z_out[j, g], z_in[way, slot, g]).astype(BF)

                z_copy(j).start()
        if step == 3:
            total_1[...] = add(part[t], own_part[...])
            for way, here in ((0, t > 0), (1, t < 3)):

                @pl.when(here)
                def _():
                    line_landed(n_in, n_out, n_recv, n_send, t, way)
                    total_1[...] += n_in[way, t].astype(F32)

            s_buf[0] = small[...]
            upstream = total_1[...]
            s_buf[0, 8:9, :] = jnp.sum(upstream * plain[...], axis=0, keepdims=True)
            s_buf[0, 9:10, :] = jnp.sum(upstream, axis=0, keepdims=True)

    s_peers = [core_peer, x_peer, y_peer, near_peer, far_peer]

    def s_copy(k):
        return remote(s_buf.at[2 * k], s_buf.at[2 * k + 1], s_send.at[k], s_recv.at[k], s_peers[k])

    for k in range(5):
        s_copy(k).start()
        s_copy(k).wait_recv()
        if k < 4:
            s_buf[2 * k + 2] = s_buf[2 * k] + s_buf[2 * k + 1]
        else:
            total_s[...] = s_buf[2 * k] + s_buf[2 * k + 1]
    sums[...] = z_out[3].astype(F32)
    for way, here in ((0, t > 0), (1, t < 3)):

        @pl.when(here)
        def _():
            line_landed(z_in, z_out, z_recv, z_send, t, way)

            @pl.loop(0, 3)
            def _(g):
                sums[g] += z_in[way, t, g].astype(F32)

    for j in range(4):
        for copy in core_copies(j) + a_copies(j) + b_copies(j):
            copy.wait_send()
        if j < 3:
            z_copy(j).wait_send()
            n_copy(j).wait_send()
    for k in range(5):
        s_copy(k).wait_send()


def scatter_all(grads, part, own_part, plain, small):
    width = part.shape[1]
    if (lax.axis_size("dp"), lax.axis_size("tensor")) != (8, 4):
        sums = [
            lax.psum_scatter(g.reshape(-1, width), ALL, scatter_dimension=0, tiled=True).astype(F32)
            for g in grads
        ]
        total = own_part + lax.psum_scatter(
            part, "tensor", scatter_dimension=0, tiled=True
        ).astype(F32)
        small = small.at[8].set(jnp.sum(total * plain, axis=0)).at[9].set(jnp.sum(total, axis=0))
        return sums, total, lax.psum(small, ALL)
    rows = grads[0].shape[1] // 8
    grads = [g.reshape(4, 2, 2, 2, rows, width) for g in grads]
    part = part.reshape(4, -1, width)
    block = part.shape[1:]
    dma = pltpu.SemaphoreType.DMA
    vmem = pl.BlockSpec(memory_space=pltpu.VMEM)
    sums, total, small = pl.pallas_call(
        scatter_kernel,
        out_shape=[
            jax.ShapeDtypeStruct((3, rows, width), F32),
            jax.ShapeDtypeStruct(block, F32),
            jax.ShapeDtypeStruct(small.shape, F32),
        ],
        in_specs=[vmem] * 7,
        out_specs=[vmem] * 3,
        scratch_shapes=[
            pltpu.VMEM((4, 3, 2, 2, rows, width), BF),
            pltpu.VMEM((4, 3, 2, rows // 2, width), BF),
            pltpu.VMEM((4, 3, 2, rows // 2, width), BF),
            pltpu.VMEM((4, 3, rows, width), BF),
            pltpu.VMEM((2, 4, 3, rows, width), BF),
            pltpu.VMEM((4, 3, rows, width), BF),
            pltpu.VMEM((2, 4) + block, BF),
            pltpu.VMEM((3,) + block, BF),
            pltpu.VMEM((10,) + small.shape, F32),
            dma((4, 7)),
            dma((4, 7)),
            dma((4,)),
            dma((2, 4)),
            dma((3,)),
            dma((2, 4)),
            dma((5,)),
            dma((5,)),
        ],
        compiler_params=pltpu.CompilerParams(
            collective_id=1, has_side_effects=True, vmem_limit_bytes=52 * 1024 * 1024
        ),
    )(*grads, part, own_part, plain, small)
    return [sums[0], sums[1], sums[2]], total, small


def local(
    block_input,
    w_q,
    w_k,
    w_v,
    w_o,
    b_q,
    b_v,
    b_o,
    w_1,
    b_1,
    w_2,
    b_2,
    gain_1,
    shift_1,
    gain_2,
    shift_2,
    cotangent,
):
    inputs = block_input[0].astype(F32)
    width = inputs.shape[1]
    cols = w_q.shape[1]
    normed_1, plain_1, inverse_1 = normalize(inputs, gain_1, shift_1)
    own_1 = normed_1.astype(BF)
    shards = [jnp.concatenate([w_q, w_k, w_v, w_o.T], axis=1), w_1, w_2.T]
    (packed, up_w, down_wt), full_1, biases = gather_all(
        shards, own_1, jnp.concatenate([b_q, b_v, b_1])
    )
    query_w, key_w, value_w, out_wt = (packed[:, :, i * cols : (i + 1) * cols] for i in range(4))
    bias_q = biases[:, None, :cols]
    bias_v = biases[:, None, cols : 2 * cols]
    bias_1 = biases[:, 2 * cols : 2 * cols + w_1.shape[1]]

    query = (einsum("fd,tdc->tfc", own_1, query_w) + bias_q).astype(BF)
    key = einsum("fd,tdc->tfc", full_1, key_w).astype(BF)
    value = (einsum("fd,tdc->tfc", full_1, value_w) + bias_v).astype(BF)
    mixed, totals = attend_forward(query, key, value)
    middle = inputs + einsum("tfc,tdc->fd", mixed, out_wt) + b_o
    normed_2, plain_2, inverse_2 = normalize(middle, gain_2, shift_2)
    own_2 = normed_2.astype(BF)
    hidden = einsum("fd,tdc->tfc", own_2, up_w) + bias_1[:, None, :]
    cdf = 0.5 * (1.0 + lax.erf(hidden * 0.7071067811865476))
    active = (hidden * cdf).astype(BF)
    result = middle + einsum("tfc,tdc->fd", active, down_wt) + b_2
    upstream = cotangent[0]
    grad_active = einsum("fd,tdc->tfc", upstream, down_wt)
    pdf = jnp.exp(-0.5 * hidden * hidden) * 0.3989422804014327
    grad_hidden = (grad_active * (cdf + hidden * pdf)).astype(BF)
    grad_up = einsum("fd,tfc->tdc", own_2, grad_hidden).astype(BF)
    grad_down = einsum("fd,tfc->tdc", upstream, active).astype(BF)
    sum_1 = jnp.sum(grad_hidden.astype(F32), axis=1).reshape(-1)
    grad_norm_2 = einsum("tfc,tdc->fd", grad_hidden, up_w)
    down_in = upstream.astype(F32)
    grad_mid_norm, gain2_grad, shift2_grad = normalize_back(grad_norm_2, plain_2, inverse_2, gain_2)
    grad_middle = down_in + grad_mid_norm
    grad_mid = grad_middle.astype(BF)
    grad_mixed = einsum("fd,tdc->tfc", grad_mid, out_wt).astype(BF)
    grad_query, grad_key, grad_value = attend_backward(query, key, value, grad_mixed, totals)
    part = einsum("tfc,tdc->fd", grad_key, key_w) + einsum("tfc,tdc->fd", grad_value, value_w)
    own_part = einsum("tfc,tdc->fd", grad_query, query_w)
    grad_att = [
        einsum("fd,tfc->tdc", own_1, grad_query),
        einsum("fd,tfc->tdc", full_1, grad_key),
        einsum("fd,tfc->tdc", full_1, grad_value),
        einsum("fd,tfc->tdc", grad_mid, mixed),
    ]
    grad_att = jnp.concatenate([g.astype(BF) for g in grad_att], axis=2)
    zero = jnp.zeros((1, width), F32)
    pieces = [
        jnp.sum(grad_query.astype(F32), axis=1),
        jnp.sum(grad_value.astype(F32), axis=1),
        jnp.sum(grad_middle, axis=0),
        sum_1,
        jnp.sum(down_in, axis=0),
        zero,
        zero,
        gain2_grad,
        shift2_grad,
    ]
    small = jnp.concatenate([piece.reshape(-1, width) for piece in pieces])
    small = jnp.pad(small, ((0, -small.shape[0] % 8), (0, 0)))
    (shard, shard_up, shard_down), grad_norm_1, sums = scatter_all(
        [grad_att, grad_up, grad_down], part.astype(BF), own_part, plain_1, small
    )
    shard_qw, shard_kw, shard_vw, shard_ow = jnp.split(shard, 4, axis=1)
    shard_down = shard_down.T
    grad_in_norm = normalize_back(grad_norm_1, plain_1, inverse_1, gain_1)[0]
    grad_input = grad_middle + grad_in_norm
    sum_bq, sum_bv, sum_bo, sum_b2 = sums[0], sums[1], sums[2], sums[7]
    sum_b1 = sums[3:7].reshape(-1)
    sum_g1, sum_s1, sum_g2, sum_s2 = sums[8], sums[9], sums[10], sums[11]
    return (
        result.astype(BF)[None],
        grad_input.astype(BF)[None],
        shard_qw,
        shard_kw,
        shard_vw,
        shard_ow.T,
        sum_bq,
        sum_bv,
        sum_bo,
        shard_up,
        sum_b1,
        shard_down,
        sum_b2,
        sum_g1,
        sum_s1,
        sum_g2,
        sum_s2,
    )


def solution(mesh):
    in_specs = (
        P("dp", "tensor", None),
        P("dp", "tensor"),
        P("dp", "tensor"),
        P("dp", "tensor"),
        P("tensor", "dp"),
        P("tensor"),
        P("tensor"),
        P(),
        P("dp", "tensor"),
        P("tensor"),
        P("tensor", "dp"),
        P(),
        P(),
        P(),
        P(),
        P(),
        P("dp", "tensor", None),
    )
    out_specs = (
        P("dp", "tensor", None),
        P("dp", "tensor", None),
        P("dp", "tensor"),
        P("dp", "tensor"),
        P("dp", "tensor"),
        P("tensor", "dp"),
        P(),
        P(),
        P(),
        P("dp", "tensor"),
        P(),
        P("tensor", "dp"),
        P(),
        P(),
        P(),
        P(),
        P(),
    )
    return jax.shard_map(local, mesh=mesh, in_specs=in_specs, out_specs=out_specs, check_vma=False)
```

```python
import jax
import jax.numpy as jnp
from jax import lax
from jax.experimental import pallas as pl
from jax.experimental.pallas import tpu as pltpu
from jax.sharding import PartitionSpec as P

HEAD = 64
EPS = 1e-05
BF = jnp.bfloat16
F32 = jnp.float32


def normalize(activity, gain_vec, shift_vec):
    average = jnp.mean(activity, axis=-1, keepdims=True)
    centred = activity - average
    inverse = lax.rsqrt(jnp.mean(centred * centred, axis=-1, keepdims=True) + EPS)
    normed = centred * inverse
    return (normed * gain_vec + shift_vec, normed, inverse)


def normalize_back(upstream, normed, inverse, gain_vec):
    scaled = upstream * gain_vec
    first = jnp.mean(scaled, axis=-1, keepdims=True)
    second = jnp.mean(scaled * normed, axis=-1, keepdims=True)
    grad_in = inverse * (scaled - first - normed * second)
    return (grad_in, jnp.sum(upstream * normed, axis=0), jnp.sum(upstream, axis=0))


def einsum(spec, left_side, right_side):
    return jnp.einsum(spec, left_side, right_side, preferred_element_type=F32)


def heads(activity):
    return activity.reshape(activity.shape[:2] + (-1, HEAD))


def attend_forward(query, key, value):
    scale = HEAD ** (-0.5)
    scores = einsum("tqhd,tkhd->thqk", heads(query), heads(key)) * scale
    peak = jnp.max(scores, axis=-1, keepdims=True)
    exp_scores = jnp.exp(scores - peak)
    total = jnp.sum(exp_scores, axis=-1, keepdims=True)
    mixed = einsum("thqk,tkhd->tqhd", exp_scores.astype(BF), heads(value))
    mixed = mixed / total.transpose(0, 2, 1, 3)
    return mixed.reshape(query.shape).astype(BF), peak + jnp.log(total)


def attend_backward(query, key, value, grad_mixed, totals):
    scale = HEAD ** (-0.5)
    query_h, key_h, value_h, grad_h = map(heads, (query, key, value, grad_mixed))
    probs = jnp.exp(einsum("tqhd,tkhd->thqk", query_h, key_h) * scale - totals)
    grad_value = einsum("thqk,tqhd->tkhd", probs.astype(BF), grad_h)
    grad_probs = einsum("tqhd,tkhd->thqk", grad_h, value_h)
    inner = jnp.sum(probs * grad_probs, axis=-1, keepdims=True)
    grad_scores = (probs * (grad_probs - inner)).astype(BF)
    grad_query = einsum("thqk,tkhd->tqhd", grad_scores, key_h) * scale
    grad_key = einsum("thqk,tqhd->tkhd", grad_scores, query_h) * scale
    return (
        grad_query.reshape(query.shape).astype(BF),
        grad_key.reshape(key.shape).astype(BF),
        grad_value.reshape(key.shape).astype(BF),
    )


ALL = ("tensor", "dp")
MESH = pl.DeviceIdType.MESH


def place():
    d, t = lax.axis_index("dp"), lax.axis_index("tensor")
    return d, t, d // 4, (d // 2) % 2, d % 2


def slot_order(t):
    far = jnp.where(t < 2, 3, 0)
    second = jnp.where(t == 0, 1, jnp.where(t == 3, 2, t - 1))
    third = jnp.where(t == 0, 2, jnp.where(t == 3, 1, t + 1))
    return [t, second, third, far]


def greet(peers, t, extra):
    barrier = pltpu.get_barrier_semaphore()
    for peer in peers:
        pl.semaphore_signal(barrier, inc=1, device_id=peer, device_id_type=MESH)
    d = lax.axis_index("dp")

    @pl.when(t > 0)
    def _():
        pl.semaphore_signal(barrier, inc=1, device_id=(d, t - 1), device_id_type=MESH)

    @pl.when(t < 3)
    def _():
        pl.semaphore_signal(barrier, inc=1, device_id=(d, t + 1), device_id_type=MESH)

    pl.semaphore_wait(
        barrier, len(peers) + jnp.where(t > 0, 1, 0) + jnp.where(t < 3, 1, 0)
    )


def remote(src, dst, send, recv, peer):
    return pltpu.make_async_remote_copy(
        src_ref=src, dst_ref=dst, send_sem=send, recv_sem=recv, device_id=peer, device_id_type=MESH
    )


def gather_kernel(*refs):
    ins, finals, outs = refs[:5], refs[5:10], refs[10:15]
    local_sem, out_sem, line_send, line_recv, send, recv = refs[15:]
    d, t, y, x, c = place()
    weights = outs[:3]
    half = ins[0].shape[0] // 2
    first, last = pl.ds(0, half), pl.ds(half, half)
    x_peer = (d + 2 - 4 * x, t)
    y_peer = (d + 4 - 8 * y, t)
    core_peer = (d + 1 - 2 * c, t)

    own = [out.at[t, y, x, c] for out in weights] + [out.at[t] for out in outs[3:]]
    copies = [pltpu.make_async_copy(a, b, local_sem.at[i]) for i, (a, b) in enumerate(zip(ins, own))]
    for copy in copies:
        copy.start()
    greet([x_peer, y_peer, core_peer], t, 0)
    for copy in copies:
        copy.wait()
    order = slot_order(t)

    def line(slot, way, part):
        peer = (d, jnp.minimum(t + 1, 3)) if way == 0 else (d, jnp.maximum(t - 1, 0))
        spots = [outs[3].at[slot], outs[4].at[slot]] + [out.at[slot, y, x, c] for out in weights]
        return [
            remote(spot, spot, line_send.at[way, slot, i], line_recv.at[slot, i], peer)
            for i, spot in enumerate(spots)
            if (i < 2) == (part == 1)
        ]

    def plane(slot, stage):
        made = []
        for g, out in enumerate(weights):
            if stage == 0:
                spots = [(0, out.at[slot, y, x, c, first], x_peer), (1, out.at[slot, y, x, c, last], y_peer)]
            elif stage == 1:
                spots = [(2, out.at[slot, y, :, c, first], y_peer), (3, out.at[slot, :, x, c, last], x_peer)]
            else:
                spots = [(4, out.at[slot, :, :, c], core_peer)]
            for k, spot, peer in spots:
                made.append(remote(spot, spot, send.at[slot, g, k], recv.at[slot, g, k], peer))
        return made

    def landed(slot, stage):
        for g, out in enumerate(weights):
            if stage == 0:
                spots = [(0, out.at[slot, y, 1 - x, c, first], x_peer), (1, out.at[slot, 1 - y, x, c, last], y_peer)]
            elif stage == 1:
                spots = [(2, out.at[slot, 1 - y, :, c, first], y_peer), (3, out.at[slot, :, 1 - x, c, last], x_peer)]
            else:
                spots = [(4, out.at[slot, :, :, 1 - c], core_peer)]
            for k, spot, peer in spots:
                remote(spot, spot, send.at[slot, g, k], recv.at[slot, g, k], peer).wait_recv()

    def both_ways(slot, part, act):
        @pl.when((slot <= t) & (t < 3))
        def _():
            for copy in line(slot, 0, part):
                act(copy)

        @pl.when((slot >= t) & (t > 0))
        def _():
            for copy in line(slot, 1, part):
                act(copy)

    def leave(slot):
        return [
            pltpu.make_async_copy(out.at[slot], final.at[slot], out_sem.at[slot, g])
            for g, (out, final) in enumerate(zip(weights, finals[:3]))
        ]

    def arrive(slot, part, own):
        if not own:
            for copy in line(slot, 0, part):
                copy.wait_recv()
        both_ways(slot, part, lambda copy: copy.start())

    for step in range(7):
        if step < 4:
            slot = order[step]
            arrive(slot, 0, step == 0)
            for copy in plane(slot, 0):
                copy.start()
        for stage in (0, 1):
            if 0 <= step - 1 - stage < 4:
                slot = order[step - 1 - stage]
                landed(slot, stage)
                for copy in plane(slot, stage + 1):
                    copy.start()
        if 0 <= step - 1 < 4:
            arrive(order[step - 1], 1, step == 1)
        if 0 <= step - 3:
            landed(order[step - 3], 2)
            for copy in leave(order[step - 3]):
                copy.start()
    rest = [pltpu.make_async_copy(outs[i], finals[i], local_sem.at[i]) for i in (3, 4)]
    for copy in rest:
        copy.start()
    for slot in order:
        for part in (0, 1):
            both_ways(slot, part, lambda copy: copy.wait_send())
        for stage in range(3):
            for copy in plane(slot, stage):
                copy.wait_send()
        for copy in leave(slot):
            copy.wait()
    for copy in rest:
        copy.wait()


def gather_all(shards, own_1, bias):
    rows, width = shards[0].shape
    if (lax.axis_size("dp"), lax.axis_size("tensor")) != (8, 4):
        count = lax.axis_size("tensor")
        full = [lax.all_gather(w, ALL, axis=0, tiled=True).reshape(count, -1, width) for w in shards]
        return full, lax.all_gather(own_1, "tensor", axis=0, tiled=True), lax.all_gather(
            bias, "tensor", axis=0
        )
    any_spec = pl.BlockSpec(memory_space=pl.ANY)
    bias = jnp.pad(bias, (0, -bias.shape[0] % 1024)).reshape(-1, 128)
    dma = pltpu.SemaphoreType.DMA
    shapes = [((4, 2, 2, 2, rows, width), BF)] * 3
    shapes += [((4,) + own_1.shape, BF), ((4,) + bias.shape, F32)]
    outs = pl.pallas_call(
        gather_kernel,
        out_shape=[jax.ShapeDtypeStruct(*shape) for shape in shapes],
        in_specs=[any_spec] * 5,
        out_specs=[any_spec] * 5,
        scratch_shapes=[pltpu.VMEM(*shape) for shape in shapes]
        + [dma((5,)), dma((4, 3)), dma((2, 4, 5)), dma((4, 5)), dma((4, 3, 5)), dma((4, 3, 5))],
        compiler_params=pltpu.CompilerParams(
            collective_id=0, has_side_effects=True, vmem_limit_bytes=18 * 1024 * 1024
        ),
    )(*shards, own_1, bias)
    full = [w.reshape(4, 8 * rows, width) for w in outs[:3]]
    return full, outs[3].reshape(-1, width), outs[4].reshape(4, -1)


def scatter_kernel(*refs):
    grads, (part, own_part, plain, small) = refs[:3], refs[3:7]
    sums, total_1, total_s = refs[7:10]
    r1, ra0, ra1, rb, z_in, z_out, n_in, n_out, s_buf, mine = refs[10:20]
    send, recv, z_send, z_recv, n_send, n_recv, s_send, s_recv, m_sem = refs[20:]
    d, t, y, x, c = place()
    rows = sums.shape[1]
    half = rows // 2
    first, last = pl.ds(0, half), pl.ds(half, half)
    x_peer = (d + 2 - 4 * x, t)
    y_peer = (d + 4 - 8 * y, t)
    core_peer = (d + 1 - 2 * c, t)
    near_peer = (d, t + 1 - 2 * (t % 2))
    far_peer = (d, t + 2 - 4 * (t // 2))
    order = slot_order(t)[::-1]

    def own_copies(j):
        return [
            pltpu.make_async_copy(grads[g].at[order[j], :, :, c], mine.at[j, g], m_sem.at[j, g])
            for g in range(3)
        ]

    for j in range(4):
        for copy in own_copies(j):
            copy.start()
    greet([x_peer, y_peer, core_peer, far_peer], t, 0)

    def core_copies(j):
        slot = order[j]
        return [
            remote(grads[g].at[slot, :, :, 1 - c], r1.at[j, g], send.at[j, g], recv.at[j, g], core_peer)
            for g in range(3)
        ]

    def a_copies(j):
        return [
            remote(r1.at[j, :, 1 - y, :, first], ra0.at[j], send.at[j, 3], recv.at[j, 3], y_peer),
            remote(r1.at[j, :, :, 1 - x, last], ra1.at[j], send.at[j, 4], recv.at[j, 4], x_peer),
        ]

    def b_copies(j):
        return [
            remote(ra0.at[j, :, 1 - x], rb.at[j, :, first], send.at[j, 5], recv.at[j, 5], x_peer),
            remote(ra1.at[j, :, 1 - y], rb.at[j, :, last], send.at[j, 6], recv.at[j, 6], y_peer),
        ]

    def ahead(slot):
        return jnp.where(slot > t, t + 1, t - 1), jnp.where(slot > t, 0, 1)

    def z_copy(j):
        slot = order[j]
        peer, way = ahead(slot)
        return remote(z_out.at[j], z_in.at[way, slot], z_send.at[j], z_recv.at[way, slot], (d, peer))

    def n_copy(j):
        slot = order[j]
        peer, way = ahead(slot)
        return remote(n_out.at[j], n_in.at[way, slot], n_send.at[j], n_recv.at[way, slot], (d, peer))

    def line_landed(buf, out, sem, peer_sem, slot, way):
        remote(out.at[0], buf.at[way, slot], peer_sem.at[0], sem.at[way, slot], near_peer).wait_recv()

    def add(a, b):
        return a.astype(F32) + b.astype(F32)

    s_peers = [core_peer, x_peer, y_peer, near_peer, far_peer]

    def s_copy(k):
        return remote(s_buf.at[2 * k], s_buf.at[2 * k + 1], s_send.at[k], s_recv.at[k], s_peers[k])

    def s_step(k):
        s_copy(k).wait_recv()
        if k < 4:
            s_buf[2 * k + 2] = s_buf[2 * k] + s_buf[2 * k + 1]
            s_copy(k + 1).start()
        else:
            total_s[...] = s_buf[2 * k] + s_buf[2 * k + 1]

    for j in range(4):
        for copy in core_copies(j):
            copy.start()
    for step in range(6):
        if step < 3:
            slot = order[step]
            way = jnp.where(slot > t, 0, 1)
            fed = ((slot > t) & (t > 0)) | ((slot < t) & (t < 3))

            @pl.when(fed)
            def _():
                line_landed(n_in, n_out, n_recv, n_send, slot, way)
                n_out[step] = add(part[slot], n_in[way, slot]).astype(BF)

            @pl.when(jnp.logical_not(fed))
            def _():
                n_out[step] = part[slot]

            n_copy(step).start()
        if step < 4:
            j = step
            for copy in own_copies(j):
                copy.wait()
            for copy in core_copies(j):
                copy.wait_recv()

            @pl.loop(0, 4)
            def _(m):
                for g in range(3):
                    r1[j, g, m // 2, m % 2] = add(
                        r1[j, g, m // 2, m % 2], mine[j, g, m // 2, m % 2]
                    ).astype(BF)

            for copy in a_copies(j):
                copy.start()
        if 0 <= step - 1 < 4:
            j = step - 1
            for copy in a_copies(j):
                copy.wait_recv()

            @pl.loop(0, 2)
            def _(m):
                for g in range(3):
                    ra0[j, g, m] = add(ra0[j, g, m], r1[j, g, y, m, first]).astype(BF)
                    ra1[j, g, m] = add(ra1[j, g, m], r1[j, g, m, x, last]).astype(BF)

            for copy in b_copies(j):
                copy.start()
        if 0 <= step - 2 < 4:
            j = step - 2
            slot = order[j]
            for copy in b_copies(j):
                copy.wait_recv()

            @pl.loop(0, 3)
            def _(g):
                z_out[j, g, first] = add(rb[j, g, first], ra0[j, g, x]).astype(BF)
                z_out[j, g, last] = add(rb[j, g, last], ra1[j, g, y]).astype(BF)

            if j < 3:
                way = jnp.where(slot > t, 0, 1)
                fed = ((slot > t) & (t > 0)) | ((slot < t) & (t < 3))

                @pl.when(fed)
                def _():
                    line_landed(z_in, z_out, z_recv, z_send, slot, way)

                    @pl.loop(0, 3)
                    def _(g):
                        z_out[j, g] = add(z_out[j, g], z_in[way, slot, g]).astype(BF)

                z_copy(j).start()
        if step == 3:
            total_1[...] = add(part[t], own_part[...])
            for way, here in ((0, t > 0), (1, t < 3)):

                @pl.when(here)
                def _():
                    line_landed(n_in, n_out, n_recv, n_send, t, way)
                    total_1[...] += n_in[way, t].astype(F32)

            s_buf[0] = small[...]
            upstream = total_1[...]
            s_buf[0, 8:9, :] = jnp.sum(upstream * plain[...], axis=0, keepdims=True)
            s_buf[0, 9:10, :] = jnp.sum(upstream, axis=0, keepdims=True)
            s_copy(0).start()
        if step > 3:
            s_step(step - 4)

    s_step(2)
    sums[...] = z_out[3].astype(F32)
    s_step(3)
    for way, here in ((0, t > 0), (1, t < 3)):

        @pl.when(here)
        def _():
            line_landed(z_in, z_out, z_recv, z_send, t, way)

            @pl.loop(0, 3)
            def _(g):
                sums[g] += z_in[way, t, g].astype(F32)

    s_step(4)
    for j in range(4):
        for copy in core_copies(j) + a_copies(j) + b_copies(j):
            copy.wait_send()
        if j < 3:
            z_copy(j).wait_send()
            n_copy(j).wait_send()
    for k in range(5):
        s_copy(k).wait_send()


def scatter_all(grads, part, own_part, plain, small):
    width = part.shape[1]
    if (lax.axis_size("dp"), lax.axis_size("tensor")) != (8, 4):
        sums = [
            lax.psum_scatter(g.reshape(-1, width), ALL, scatter_dimension=0, tiled=True).astype(F32)
            for g in grads
        ]
        total = own_part + lax.psum_scatter(
            part, "tensor", scatter_dimension=0, tiled=True
        ).astype(F32)
        small = small.at[8].set(jnp.sum(total * plain, axis=0)).at[9].set(jnp.sum(total, axis=0))
        return sums, total, lax.psum(small, ALL)
    rows = grads[0].shape[1] // 8
    grads = [g.reshape(4, 2, 2, 2, rows, width) for g in grads]
    part = part.reshape(4, -1, width)
    block = part.shape[1:]
    dma = pltpu.SemaphoreType.DMA
    vmem = pl.BlockSpec(memory_space=pltpu.VMEM)
    sums, total, small = pl.pallas_call(
        scatter_kernel,
        out_shape=[
            jax.ShapeDtypeStruct((3, rows, width), F32),
            jax.ShapeDtypeStruct(block, F32),
            jax.ShapeDtypeStruct(small.shape, F32),
        ],
        in_specs=[pl.BlockSpec(memory_space=pl.ANY)] * 3 + [vmem] * 4,
        out_specs=[vmem] * 3,
        scratch_shapes=[
            pltpu.VMEM((4, 3, 2, 2, rows, width), BF),
            pltpu.VMEM((4, 3, 2, rows // 2, width), BF),
            pltpu.VMEM((4, 3, 2, rows // 2, width), BF),
            pltpu.VMEM((4, 3, rows, width), BF),
            pltpu.VMEM((2, 4, 3, rows, width), BF),
            pltpu.VMEM((4, 3, rows, width), BF),
            pltpu.VMEM((2, 4) + block, BF),
            pltpu.VMEM((3,) + block, BF),
            pltpu.VMEM((10,) + small.shape, F32),
            pltpu.VMEM((4, 3, 2, 2, rows, width), BF),
            dma((4, 7)),
            dma((4, 7)),
            dma((4,)),
            dma((2, 4)),
            dma((3,)),
            dma((2, 4)),
            dma((5,)),
            dma((5,)),
            dma((4, 3)),
        ],
        compiler_params=pltpu.CompilerParams(
            collective_id=1, has_side_effects=True, vmem_limit_bytes=38 * 1024 * 1024
        ),
    )(*grads, part, own_part, plain, small)
    return [sums[0], sums[1], sums[2]], total, small


def local(
    block_input,
    w_q,
    w_k,
    w_v,
    w_o,
    b_q,
    b_v,
    b_o,
    w_1,
    b_1,
    w_2,
    b_2,
    gain_1,
    shift_1,
    gain_2,
    shift_2,
    cotangent,
):
    inputs = block_input[0].astype(F32)
    width = inputs.shape[1]
    cols = w_q.shape[1]
    normed_1, plain_1, inverse_1 = normalize(inputs, gain_1, shift_1)
    own_1 = normed_1.astype(BF)
    shards = [jnp.concatenate([w_q, w_k, w_v, w_o.T], axis=1), w_1, w_2.T]
    (packed, up_w, down_wt), full_1, biases = gather_all(
        shards, own_1, jnp.concatenate([b_q, b_v, b_1])
    )
    query_w, key_w, value_w, out_wt = (packed[:, :, i * cols : (i + 1) * cols] for i in range(4))
    bias_q = biases[:, None, :cols]
    bias_v = biases[:, None, cols : 2 * cols]
    bias_1 = biases[:, 2 * cols : 2 * cols + w_1.shape[1]]

    query = (einsum("fd,tdc->tfc", own_1, query_w) + bias_q).astype(BF)
    key = einsum("fd,tdc->tfc", full_1, key_w).astype(BF)
    value = (einsum("fd,tdc->tfc", full_1, value_w) + bias_v).astype(BF)
    mixed, totals = attend_forward(query, key, value)
    middle = inputs + einsum("tfc,tdc->fd", mixed, out_wt) + b_o
    normed_2, plain_2, inverse_2 = normalize(middle, gain_2, shift_2)
    own_2 = normed_2.astype(BF)
    hidden = einsum("fd,tdc->tfc", own_2, up_w) + bias_1[:, None, :]
    cdf = 0.5 * (1.0 + lax.erf(hidden * 0.7071067811865476))
    active = (hidden * cdf).astype(BF)
    result = middle + einsum("tfc,tdc->fd", active, down_wt) + b_2
    upstream = cotangent[0]
    grad_active = einsum("fd,tdc->tfc", upstream, down_wt)
    pdf = jnp.exp(-0.5 * hidden * hidden) * 0.3989422804014327
    grad_hidden = (grad_active * (cdf + hidden * pdf)).astype(BF)
    grad_up = einsum("fd,tfc->tdc", own_2, grad_hidden).astype(BF)
    grad_down = einsum("fd,tfc->tdc", upstream, active).astype(BF)
    sum_1 = jnp.sum(grad_hidden.astype(F32), axis=1).reshape(-1)
    grad_norm_2 = einsum("tfc,tdc->fd", grad_hidden, up_w)
    down_in = upstream.astype(F32)
    grad_mid_norm, gain2_grad, shift2_grad = normalize_back(grad_norm_2, plain_2, inverse_2, gain_2)
    grad_middle = down_in + grad_mid_norm
    grad_mid = grad_middle.astype(BF)
    grad_mixed = einsum("fd,tdc->tfc", grad_mid, out_wt).astype(BF)
    grad_query, grad_key, grad_value = attend_backward(query, key, value, grad_mixed, totals)
    part = einsum("tfc,tdc->fd", grad_key, key_w) + einsum("tfc,tdc->fd", grad_value, value_w)
    own_part = einsum("tfc,tdc->fd", grad_query, query_w)
    grad_att = [
        einsum("fd,tfc->tdc", own_1, grad_query),
        einsum("fd,tfc->tdc", full_1, grad_key),
        einsum("fd,tfc->tdc", full_1, grad_value),
        einsum("fd,tfc->tdc", grad_mid, mixed),
    ]
    grad_att = jnp.concatenate([g.astype(BF) for g in grad_att], axis=2)
    zero = jnp.zeros((1, width), F32)
    pieces = [
        jnp.sum(grad_query.astype(F32), axis=1),
        jnp.sum(grad_value.astype(F32), axis=1),
        jnp.sum(grad_middle, axis=0),
        sum_1,
        jnp.sum(down_in, axis=0),
        zero,
        zero,
        gain2_grad,
        shift2_grad,
    ]
    small = jnp.concatenate([piece.reshape(-1, width) for piece in pieces])
    small = jnp.pad(small, ((0, -small.shape[0] % 8), (0, 0)))
    (shard, shard_up, shard_down), grad_norm_1, sums = scatter_all(
        [grad_att, grad_up, grad_down], part.astype(BF), own_part, plain_1, small
    )
    shard_qw, shard_kw, shard_vw, shard_ow = jnp.split(shard, 4, axis=1)
    shard_down = shard_down.T
    grad_in_norm = normalize_back(grad_norm_1, plain_1, inverse_1, gain_1)[0]
    grad_input = grad_middle + grad_in_norm
    sum_bq, sum_bv, sum_bo, sum_b2 = sums[0], sums[1], sums[2], sums[7]
    sum_b1 = sums[3:7].reshape(-1)
    sum_g1, sum_s1, sum_g2, sum_s2 = sums[8], sums[9], sums[10], sums[11]
    return (
        result.astype(BF)[None],
        grad_input.astype(BF)[None],
        shard_qw,
        shard_kw,
        shard_vw,
        shard_ow.T,
        sum_bq,
        sum_bv,
        sum_bo,
        shard_up,
        sum_b1,
        shard_down,
        sum_b2,
        sum_g1,
        sum_s1,
        sum_g2,
        sum_s2,
    )


def solution(mesh):
    in_specs = (
        P("dp", "tensor", None),
        P("dp", "tensor"),
        P("dp", "tensor"),
        P("dp", "tensor"),
        P("tensor", "dp"),
        P("tensor"),
        P("tensor"),
        P(),
        P("dp", "tensor"),
        P("tensor"),
        P("tensor", "dp"),
        P(),
        P(),
        P(),
        P(),
        P(),
        P("dp", "tensor", None),
    )
    out_specs = (
        P("dp", "tensor", None),
        P("dp", "tensor", None),
        P("dp", "tensor"),
        P("dp", "tensor"),
        P("dp", "tensor"),
        P("tensor", "dp"),
        P(),
        P(),
        P(),
        P("dp", "tensor"),
        P(),
        P("tensor", "dp"),
        P(),
        P(),
        P(),
        P(),
        P(),
    )
    return jax.shard_map(local, mesh=mesh, in_specs=in_specs, out_specs=out_specs, check_vma=False)
```
